256 devices in a mesh: row: 16 (over y_lo, x, core), col: 16 (over y_hi, z).
Axes of the slice: x: 4, y: 4 (y_hi: 2, y_lo: 2; y = y_hi * 2 + y_lo), z: 8, core: 2. Of those that a mesh axis runs over, the one named last changes fastest.
Arguments:
- start_modes: float32 [32, 131072], P(None, ('row', 'col')), may hold values from -6 to 6
- energies: float32 [131072], P(('row', 'col')), may hold values from -0.5 to 0.5
- coupling: float32 [2048, 80, 4096], P('row', 'col'), may hold values from -0.0390625 to 0.0390625
- pattern: int32 [2048, 80], P('row', 'col'), may hold values from 0 to 2047, as said below
Outputs:
- filtered: float32 [32, 131072], P(None, ('row', 'col'))
- previous: float32 [32, 131072], P(None, ('row', 'col'))
The draws below stay inside these ranges and needn't reach their ends.
Inputs may be any that keep to these rules, and one draw needn't show every extreme that they name: In block row i, the 5 entries pattern[i, c * 5] to pattern[i, c * 5 + 4] are distinct block columns j with (j // 8) % 16 == c.
All inputs are finite; a program needn't handle non-finite values.
Results may differ from the reference program's by a relative error of at most 0.0001.
Values sent between devices are 32-bit elements; how exact they have to be, the bound alone decides.
No kernel may reach another device: no remote copies, remote signals or barrier semaphores. Data moves between devices by JAX's collectives and lax.ppermute only.
A program may use at most 128 MiB of HBM per device.

```python
import jax
import jax.numpy as jnp
from jax import lax

BASIS = 131072
BLOCK = 64
SLOTS = 5
MODES = 32
DEGREE = 3
BLOCKS = 2048
COUPLED = 80
N_ROW = 16
N_COL = 16


def draw_pattern(key, part):
    block_count = BASIS // BLOCK
    group_size = block_count // N_COL
    per_piece = block_count // (N_ROW * N_COL)
    stride = group_size // SLOTS
    key_jitter, key_rotate = jax.random.split(key)
    jitter = jax.random.randint(key_jitter, (block_count, N_COL, SLOTS), 0, stride)
    rotate = jax.random.randint(key_rotate, (block_count, N_COL, 1), 0, group_size)
    offsets = (jnp.arange(SLOTS, dtype=jnp.int32)[None, None, :] * stride + jitter + rotate) % group_size
    piece_row = offsets // per_piece
    within = offsets % per_piece
    column = jnp.arange(N_COL, dtype=jnp.int32)[None, :, None]
    return ((piece_row * N_COL + column) * per_piece + within).reshape(block_count, N_COL * SLOTS).astype(jnp.int32)


def block_scale(key, shape, pieces, low, high):
    gain, own = 1.0, jax.random.fold_in(key, 6)
    for dim, parts in pieces:
        steps = jnp.exp(jax.random.uniform(jax.random.fold_in(own, dim), (parts,), jnp.float32, low / len(pieces), high / len(pieces)))
        gain = gain * jnp.repeat(steps, shape[dim] // parts).reshape([-1 if axis == dim else 1 for axis in range(len(shape))])
    return gain


def bell_draw(key, dims, deviation, reach, cuts=(), kind=jnp.bfloat16):
    values = jax.random.normal(key, dims, jnp.float32) * deviation
    if len(cuts) > 0:
        values = block_scale(key, dims, cuts, -0.22, 0.18) * values
    return jnp.clip(values, min=-reach, max=reach).astype(kind)


def setup_inputs(seed: int = 0) -> dict:
    keys = jax.random.split(jax.random.key(seed), 5)
    start_modes = bell_draw(keys[0], (MODES, BASIS), 1.0, 6.0, ((1, 256),), jnp.float32)
    energies = jnp.clip(jax.random.uniform(keys[1], (BASIS,), jnp.float32, -0.5, 0.5) * block_scale(keys[1], (BASIS,), ((0, 256),), -0.4, 0.0), -0.5, 0.5)
    coupling = bell_draw(keys[2], (BLOCKS, COUPLED, BLOCK * BLOCK), (4 * BLOCK * COUPLED) ** -0.5, 0.0390625, ((0, 16), (1, 16)), jnp.float32)
    pattern = draw_pattern(jax.random.fold_in(keys[4], 71), 0)
    return {"start_modes": start_modes, "energies": energies, "coupling": coupling, "pattern": pattern}


def operate(vector, energies, coupling, pattern):
    mode_count = vector.shape[0]
    blocks = vector.reshape(mode_count, BLOCKS, BLOCK)
    group_rows = min(BLOCKS, 128)
    groups = BLOCKS // group_rows

    def block_rows(inputs):
        sub_mats, sub_cols = inputs
        picked = jnp.take(blocks, sub_cols.reshape(-1), axis=1).reshape(mode_count, group_rows, COUPLED, BLOCK)
        block_mats = sub_mats.reshape(group_rows, COUPLED, BLOCK, BLOCK)
        return jnp.einsum("mrsb,rsab->rma", picked, block_mats, precision=lax.Precision.HIGHEST)

    result = lax.map(block_rows, (coupling.reshape(groups, group_rows, COUPLED, BLOCK * BLOCK), pattern.reshape(groups, group_rows, COUPLED)))
    coupled = jnp.transpose(result, (2, 0, 1, 3)).reshape(mode_count, BASIS)
    return energies[None, :] * vector + coupled


def reference(start_modes, energies, coupling, pattern):
    previous = start_modes
    current = operate(start_modes, energies, coupling, pattern)
    for degree in range(DEGREE - 1):
        upcoming = 2.0 * operate(current, energies, coupling, pattern) - previous
        previous = current
        current = upcoming
    return current, previous
```

```python
import functools

import jax
import jax.numpy as jnp
from jax import lax
from jax.experimental import pallas as pl
from jax.experimental.pallas import tpu as pltpu
from jax.sharding import Mesh
from jax.sharding import PartitionSpec as P

BLOCK = 64
DEGREE = 3
LANES = 128
SUB = 8
SLOTS = 5
PAIRS = (SLOTS + 1) // 2
MODES = 32
PER_PIECE = 8
PIECE = BLOCK * PER_PIECE
TILES = PIECE // LANES
ROWS_HERE = 128
HALF_ROW = BLOCK // 2

Y_LO, X, CORE, Y_HI, Z = 2, 4, 2, 2, 8
ROW_AXES = ("y_lo", "x", "core")
COL_AXES = ("y_hi", "z")
ROW_CHIPS = ("y_lo", "x")


def split(value):
    high = value.astype(jnp.bfloat16)
    low = (value - high.astype(jnp.float32)).astype(jnp.bfloat16)
    return high, low


def left_half(shape):
    return lax.broadcasted_iota(jnp.int32, shape, len(shape) - 1) < BLOCK


def prepare_kernel(raw_ref, out_ref, rows):
    left = left_half((HALF_ROW, LANES))
    zero = jnp.zeros((HALF_ROW, LANES), jnp.float32)
    for row in range(SUB):
        for pair in range(PAIRS):
            first = raw_ref[2 * pair, 0, :, row, :]
            second = raw_ref[2 * pair + 1, 0, :, row, :] if 2 * pair + 1 < SLOTS else None
            if second is None:
                even = jnp.where(left, first, zero)
                odd = jnp.where(left, pltpu.roll(first, BLOCK, 1), zero)
            else:
                even = jnp.where(left, first, pltpu.roll(second, BLOCK, 1))
                odd = jnp.where(left, pltpu.roll(first, BLOCK, 1), second)
            slot = (row * PAIRS + pair) % 2
            rows[slot, pl.ds(0, HALF_ROW, stride=2), :] = even
            rows[slot, pl.ds(1, HALF_ROW, stride=2), :] = odd
            high, low = split(rows[slot])
            lanes = pl.ds(pair * LANES, LANES)
            out_ref[row, 0:BLOCK, lanes] = high
            out_ref[row, BLOCK : 2 * BLOCK, lanes] = low


def prepare(coupling):
    groups = ROWS_HERE // SUB
    raw = coupling.reshape(groups, SUB, SLOTS, HALF_ROW, LANES).transpose(2, 0, 3, 1, 4)
    return pl.pallas_call(
        prepare_kernel,
        grid=(groups,),
        in_specs=[pl.BlockSpec((SLOTS, 1, HALF_ROW, SUB, LANES), lambda g: (0, g, 0, 0, 0))],
        out_specs=pl.BlockSpec((SUB, 2 * BLOCK, PAIRS * LANES), lambda g: (g, 0, 0)),
        out_shape=jax.ShapeDtypeStruct((ROWS_HERE, 2 * BLOCK, PAIRS * LANES), jnp.bfloat16),
        scratch_shapes=[pltpu.VMEM((2, BLOCK, LANES), jnp.float32)],
        name="prepare",
    )(raw)


def apply_kernel(places, mine_ref, other_ref, mats_ref, out_ref, picks):
    group = pl.program_id(0)

    @pl.when(group == 0)
    def _():
        for half, ref in enumerate((mine_ref, other_ref)):
            for chip in range(Y_LO * X):
                for tile in range(TILES):
                    value = ref[chip, :, pl.ds(tile * LANES, LANES)]
                    place = (half * Y_LO * X + chip) * PER_PIECE + 2 * tile
                    for turn, turned in enumerate((value, pltpu.roll(value, BLOCK, 1))):
                        high, low = split(turned)
                        picks[place + turn, 0:MODES, :] = high
                        picks[place + turn, MODES : 2 * MODES, :] = low

    left_picks = left_half((2 * MODES, LANES))
    left_out = left_half((MODES, LANES))
    previous = None
    for row in range(SUB):
        parts = []
        for pair in range(PAIRS):
            first = places[2 * pair, group * SUB + row]
            part = picks[first]
            if 2 * pair + 1 < SLOTS:
                second = places[2 * pair + 1, group * SUB + row]
                part = jnp.where(left_picks, part, picks[second ^ 1])
            parts.append(part)
        product = lax.dot_general(
            jnp.concatenate(parts, axis=1),
            mats_ref[row],
            (((1,), (1,)), ((), ())),
            preferred_element_type=jnp.float32,
        )
        both = product[0:MODES] + product[MODES : 2 * MODES]
        both = both + pltpu.roll(both, BLOCK, 1)
        if row % 2 == 1:
            out_ref[0, :, pl.ds(row // 2 * LANES, LANES)] = jnp.where(left_out, previous, both)
        previous = both


def apply(places, mine, other, mats):
    whole = (Y_LO * X, MODES, PIECE)
    grid_spec = pltpu.PrefetchScalarGridSpec(
        num_scalar_prefetch=1,
        grid=(ROWS_HERE // SUB,),
        in_specs=[
            pl.BlockSpec(whole, lambda g, p: (0, 0, 0)),
            pl.BlockSpec(whole, lambda g, p: (0, 0, 0)),
            pl.BlockSpec((SUB, 2 * BLOCK, PAIRS * LANES), lambda g, p: (g, 0, 0)),
        ],
        out_specs=pl.BlockSpec((1, MODES, PIECE), lambda g, p: (g, 0, 0)),
        scratch_shapes=[pltpu.VMEM((ROWS_HERE, 2 * MODES, LANES), jnp.bfloat16)],
    )
    return pl.pallas_call(
        apply_kernel,
        grid_spec=grid_spec,
        out_shape=jax.ShapeDtypeStruct((Y_HI * Z, MODES, PIECE), jnp.float32),
        name="apply",
    )(places, mine, other, mats)


def swap(value, axis):
    return lax.ppermute(value, axis, [(0, 1), (1, 0)])


def shards(start_modes, energies, coupling, pattern):
    core = lax.axis_index("core")
    y_hi = lax.axis_index("y_hi")
    turned = pattern.T
    piece_row = turned // (PER_PIECE * Y_HI * Z)
    places = (((piece_row % CORE) ^ core) * (Y_LO * X) + piece_row // CORE) * PER_PIECE + turned % PER_PIECE
    mats = prepare(coupling)

    def operate(vector):
        copies = jnp.broadcast_to(vector[None], (Y_LO * X, MODES, PIECE))
        mine = lax.all_to_all(copies, ROW_CHIPS, 0, 0, tiled=False)
        other = swap(mine, "core")
        shares = apply(places, mine, other, mats).reshape(Y_HI, Z, MODES, PIECE)
        away = lax.dynamic_index_in_dim(shares, 1 - y_hi, 0, keepdims=False)
        kept = lax.dynamic_index_in_dim(shares, y_hi, 0, keepdims=False)
        kept = kept + swap(away, "y_hi")
        pieces = lax.all_to_all(kept, "z", 0, 0, tiled=False)
        return energies[None, :] * vector + jnp.sum(pieces, axis=0)

    previous = start_modes
    current = operate(start_modes)
    for degree in range(DEGREE - 1):
        upcoming = 2.0 * operate(current) - previous
        previous = current
        current = upcoming
    return (current, previous)


def solution(mesh):
    fine = Mesh(mesh.devices.reshape(Y_LO, X, CORE, Y_HI, Z), ROW_AXES + COL_AXES)
    both = ROW_AXES + COL_AXES
    in_specs = (P(None, both), P(both), P(ROW_AXES, COL_AXES, None), P(ROW_AXES, COL_AXES))
    out_specs = (P(None, both), P(None, both))
    return jax.shard_map(shards, mesh=fine, in_specs=in_specs, out_specs=out_specs, check_vma=False)
```

```python
import functools

import jax
import jax.numpy as jnp
from jax import lax
from jax.experimental import pallas as pl
from jax.experimental.pallas import tpu as pltpu
from jax.sharding import Mesh
from jax.sharding import PartitionSpec as P

BLOCK = 64
DEGREE = 3
LANES = 128
SUB = 8
SLOTS = 5
PAIRS = (SLOTS + 1) // 2
DEPTH = SLOTS * BLOCK
MODES = 32
PER_PIECE = 8
PIECE = BLOCK * PER_PIECE
TILES = PIECE // LANES
ROWS_HERE = 128
HALF_ROW = BLOCK // 2
AT_ONCE = 2

Y_LO, X, CORE, Y_HI, Z_HI, Z_LO = 2, 4, 2, 2, 4, 2
CHIPS = Y_LO * X
Z = Z_HI * Z_LO
CHUNKS = Y_HI * Z
EARLY = Z_HI // 2
ROW_AXES = ("y_lo", "x", "core")
COL_AXES = ("y_hi", "z_hi", "z_lo")
IN_VMEM = pl.BlockSpec(memory_space=pltpu.VMEM)
IN_SMEM = pl.BlockSpec(memory_space=pltpu.SMEM)


def kept_in_vmem(*shape, dtype=jnp.float32):
    return pltpu.VMEM(shape, dtype)


def call(kernel, name, in_specs, outs, scratch=(), flops=1_000_000, mebibytes=8, **more):
    return pl.pallas_call(
        kernel,
        in_specs=in_specs,
        out_specs=[IN_VMEM] * len(outs),
        out_shape=list(outs),
        scratch_shapes=list(scratch),
        compiler_params=pltpu.CompilerParams(vmem_limit_bytes=mebibytes << 20),
        cost_estimate=pl.CostEstimate(flops=flops, bytes_accessed=1 << 20, transcendentals=0),
        name=name,
        **more,
    )


def split(value):
    high = value.astype(jnp.bfloat16)
    low = (value - high.astype(jnp.float32)).astype(jnp.bfloat16)
    return high, low


def left_half(shape):
    return lax.broadcasted_iota(jnp.int32, shape, len(shape) - 1) < BLOCK


def prepare_kernel(where, places, raw_ref, out_ref, rows):
    left = left_half((HALF_ROW, LANES))
    down, across = (lax.broadcasted_iota(jnp.int32, (LANES, LANES), dim) for dim in range(2))
    unit = jnp.where(down == across, 1.0, 0.0).astype(jnp.bfloat16)
    for chunk in range(AT_ONCE):
        for row in range(SUB):
            for pair in range(PAIRS):
                first = raw_ref[2 * pair, chunk, :, row, :]
                last = 2 * pair + 1 == SLOTS
                second = first if last else raw_ref[2 * pair + 1, chunk, :, row, :]
                even = jnp.where(left, first, pltpu.roll(second, BLOCK, 1))
                odd = jnp.where(left, pltpu.roll(first, BLOCK, 1), second)
                slot = (chunk * SUB + row) * PAIRS + pair
                rows[slot, pl.ds(0, HALF_ROW, stride=2), :] = even
                rows[slot, pl.ds(1, HALF_ROW, stride=2), :] = odd
                depth = BLOCK if last else LANES
                turned = lax.dot_general(
                    unit[0:depth],
                    jnp.concatenate(split(rows[slot]), axis=0),
                    (((1,), (1,)), ((), ())),
                    preferred_element_type=jnp.float32,
                )
                out_ref[chunk, row, pl.ds(pair * LANES, depth), :] = turned.astype(jnp.bfloat16)


def prepare(where, places, coupling):
    raw = coupling.reshape(CHUNKS, SUB, SLOTS, HALF_ROW, LANES).transpose(2, 0, 3, 1, 4)
    raw = pltpu.with_memory_space_constraint(raw, pltpu.HBM)
    return pl.pallas_call(
        prepare_kernel,
        grid=(CHUNKS // AT_ONCE,),
        in_specs=[IN_SMEM, IN_SMEM, pl.BlockSpec((SLOTS, AT_ONCE, HALF_ROW, SUB, LANES), lambda g: (0, g, 0, 0, 0))],
        out_specs=pl.BlockSpec((AT_ONCE, SUB, DEPTH, LANES), lambda g: (g, 0, 0, 0)),
        out_shape=pltpu.HBM((CHUNKS, SUB, DEPTH, LANES), jnp.bfloat16),
        scratch_shapes=[pltpu.VMEM((AT_ONCE * SUB * PAIRS, BLOCK, LANES), jnp.float32)],
        compiler_params=pltpu.CompilerParams(vmem_limit_bytes=16 << 20),
        cost_estimate=pl.CostEstimate(flops=20_000_000_000, bytes_accessed=21 << 20, transcendentals=0),
        name="prepare",
    )(where, places, raw)


def fill_picks(refs, picks):
    for half, ref in enumerate(refs):
        for chip in range(CHIPS):
            for tile in range(TILES):
                value = ref[chip, :, pl.ds(tile * LANES, LANES)]
                place = (half * CHIPS + chip) * PER_PIECE + 2 * tile
                for turn, turned in enumerate((value, pltpu.roll(value, BLOCK, 1))):
                    high, low = split(turned)
                    picks[place + turn, 0:MODES, :] = high
                    picks[place + turn, MODES : 2 * MODES, :] = low


def multiply(chunks, stores, places, picks, mats):
    left_picks = left_half((2 * MODES, LANES))
    left_out = left_half((MODES, LANES))
    for chunk, store in zip(chunks, stores):
        previous = None
        for offset in range(SUB):
            row = chunk * SUB + offset
            parts = []
            for pair in range(PAIRS):
                part = picks[places[2 * pair, row]]
                if 2 * pair + 1 < SLOTS:
                    parts.append(jnp.where(left_picks, part, picks[places[2 * pair + 1, row] ^ 1]))
                else:
                    parts.append(part[:, 0:BLOCK])
            product = jnp.dot(jnp.concatenate(parts, axis=1), mats[chunk, offset], preferred_element_type=jnp.float32)
            both = product[0:MODES] + product[MODES : 2 * MODES]
            both = both + pltpu.roll(both, BLOCK, 1)
            if offset % 2 == 1:
                store(pl.ds(offset // 2 * LANES, LANES), jnp.where(left_out, previous, both))
            previous = both


def into(ref, *index):
    def store(lanes, value):
        ref[(*index, slice(None), lanes)] = value

    return store


def late_chunks(parity):
    return [(y, a, y * Z + (EARLY + a) * Z_LO + parity) for y in range(Y_HI) for a in range(Z_HI - EARLY)]


def first_kernel(where, places, mine, other, mats, out, picks):
    chunks = [(1 - where[0]) * Z + k for k in range(EARLY * Z_LO)]
    fill_picks((mine, other), picks)
    multiply(chunks, [into(out, k) for k in range(len(chunks))], places, picks, mats)


def second_kernel(where, places, picks, mats, out):
    late = late_chunks(1 - where[1])
    chunks = [chunk for _, _, chunk in late]
    multiply(chunks, [into(out, y, a) for y, a, _ in late], places, picks, mats)


def third_kernel(where, places, picks, mats, early_out, late_out):
    late = late_chunks(where[1])
    chunks = [where[0] * Z + k for k in range(EARLY * Z_LO)]
    stores = [into(early_out, k) for k in range(len(chunks))]
    chunks += [chunk for _, _, chunk in late]
    stores += [into(late_out, y, a) for y, a, _ in late]
    multiply(chunks, stores, places, picks, mats)


def multiplier(kernel, name, inputs, outs, count):
    return call(
        kernel,
        name,
        [IN_SMEM, IN_SMEM] + [IN_VMEM] * (inputs + 1),
        outs,
        flops=count * 400_000_000,
    )


def middle_kernel(where, early_kept, early_got, late_kept, late_got, beside, across, early, late):
    y, parity = where[0], where[1]
    for a in range(EARLY):
        for target, half in ((early, parity), (beside, 1 - parity)):
            target[a] = early_kept[Z_LO * a + half] + early_got[Z_LO * a + half]
    for a in range(Z_HI - EARLY):
        for target, half in ((late, y), (across, 1 - y)):
            target[a] = late_kept[half, a] + late_got[half, a]


def last_kernel(early, beside_got, late, across_got, sums):
    for a in range(EARLY):
        sums[a] = early[a] + beside_got[a]
    for a in range(Z_HI - EARLY):
        sums[EARLY + a] = late[a] + across_got[a]


def finish_kernel(scale, energies, vector, before, pieces, out, copies):
    total = energies[...] * vector[...]
    for chip in range(Z_HI):
        total = total + pieces[chip]
    if scale != 1.0:
        total = scale * total - before[...]
    out[...] = total
    for chip in range(CHIPS):
        copies[chip] = total


def tie_kernel(mine, mats, out):
    pass


def swap(value, axis):
    return lax.ppermute(value, axis, [(0, 1), (1, 0)])


def reduce(where, away, beside, early_kept, late_kept):
    away_got, beside_got = swap(away, "y_hi"), swap(beside, "z_lo")
    piece = kept_in_vmem(EARLY, MODES, PIECE)
    beside, across, early, late = call(middle_kernel, "middle", [IN_SMEM] + [IN_VMEM] * 4, [piece] * 4)(
        where, early_kept, away_got, late_kept, beside_got
    )
    beside_got, across_got = swap(beside, "z_lo"), swap(across, "y_hi")
    [sums] = call(last_kernel, "last", [IN_VMEM] * 4, [kept_in_vmem(Z_HI, MODES, PIECE)])(
        early, beside_got, late, across_got
    )
    return lax.all_to_all(sums, "z_hi", 0, 0, tiled=False)


def shards(start_modes, energies, coupling, pattern):
    core, y_hi, z_lo = (lax.axis_index(name) for name in ("core", "y_hi", "z_lo"))
    turned = pattern.T
    piece_row = turned // (PER_PIECE * CHUNKS)
    places = (((piece_row % CORE) ^ core) * CHIPS + piece_row // CORE) * PER_PIECE + turned % PER_PIECE
    where = jnp.stack([y_hi, z_lo]).astype(jnp.int32)
    mats = prepare(where, places, coupling)
    level = energies[None, :]
    picks_shape = kept_in_vmem(ROWS_HERE, 2 * MODES, LANES, dtype=jnp.bfloat16)
    early_shape = kept_in_vmem(EARLY * Z_LO, MODES, PIECE)
    late_shape = kept_in_vmem(Y_HI, Z_HI - EARLY, MODES, PIECE)

    def operate(copies, tied):
        mine = lax.all_to_all(copies, ("y_lo", "x"), 0, 0, tiled=False)
        if tied:
            [mine] = call(
                tie_kernel, "tie", [IN_VMEM, pl.BlockSpec(memory_space=pl.ANY)], [kept_in_vmem(*mine.shape)], input_output_aliases={0: 0}
            )(mine, pltpu.with_memory_space_constraint(mats, pltpu.HBM))
        other = swap(mine, "core")
        away, picks = multiplier(first_kernel, "first", 2, [early_shape, picks_shape], 4)(where, places, mine, other, mats)
        [beside] = multiplier(second_kernel, "second", 1, [late_shape], 4)(where, places, picks, mats)
        early, late = multiplier(third_kernel, "third", 1, [early_shape, late_shape], 8)(where, places, picks, mats)
        return reduce(where, away, beside, early, late)

    vector_shape = kept_in_vmem(MODES, PIECE)
    previous = before = start_modes
    current = start_modes
    copies = jnp.broadcast_to(start_modes[None], (CHIPS, MODES, PIECE))
    for degree in range(DEGREE):
        pieces = operate(copies, degree == 0)
        finish = functools.partial(finish_kernel, 1.0 if degree == 0 else 2.0)
        upcoming, copies = call(
            finish, "finish", [IN_VMEM] * 4, [vector_shape, kept_in_vmem(CHIPS, MODES, PIECE)]
        )(level, current, before, pieces)
        before = current
        current = upcoming
    return (current, before)


def solution(mesh):
    fine = Mesh(mesh.devices.reshape(Y_LO, X, CORE, Y_HI, Z_HI, Z_LO), ROW_AXES + COL_AXES)
    both = ROW_AXES + COL_AXES
    in_specs = (P(None, both), P(both), P(ROW_AXES, COL_AXES, None), P(ROW_AXES, COL_AXES))
    out_specs = (P(None, both), P(None, both))
    return jax.shard_map(shards, mesh=fine, in_specs=in_specs, out_specs=out_specs, check_vma=False)
```

```python
import functools

import jax
import jax.numpy as jnp
from jax import lax
from jax.experimental import pallas as pl
from jax.experimental.pallas import tpu as pltpu
from jax.sharding import Mesh
from jax.sharding import PartitionSpec as P

BLOCK = 64
DEGREE = 3
LANES = 128
SUB = 8
SLOTS = 5
PAIRS = (SLOTS + 1) // 2
DEPTH = SLOTS * BLOCK
MODES = 32
PER_PIECE = 8
PIECE = BLOCK * PER_PIECE
TILES = PIECE // LANES
ROWS_HERE = 128
HALF_ROW = BLOCK // 2
AT_ONCE = 2

Y_LO, X, CORE, Y_HI, Z_HI, Z_LO = 2, 4, 2, 2, 4, 2
CHIPS = Y_LO * X
Z = Z_HI * Z_LO
CHUNKS = Y_HI * Z
ROW_AXES = ("y_lo", "x", "core")
COL_AXES = ("y_hi", "z_hi", "z_lo")
IN_VMEM = pl.BlockSpec(memory_space=pltpu.VMEM)
IN_SMEM = pl.BlockSpec(memory_space=pltpu.SMEM)


def kept_in_vmem(*shape, dtype=jnp.float32):
    return pltpu.VMEM(shape, dtype)


def call(kernel, name, in_specs, outs, scratch=(), flops=1_000_000, mebibytes=8, **more):
    return pl.pallas_call(
        kernel,
        in_specs=in_specs,
        out_specs=[IN_VMEM] * len(outs),
        out_shape=list(outs),
        scratch_shapes=list(scratch),
        compiler_params=pltpu.CompilerParams(vmem_limit_bytes=mebibytes << 20),
        cost_estimate=pl.CostEstimate(flops=flops, bytes_accessed=100_000, transcendentals=0),
        name=name,
        **more,
    )


def split(value):
    high = value.astype(jnp.bfloat16)
    low = (value - high.astype(jnp.float32)).astype(jnp.bfloat16)
    return high, low


def left_half(shape):
    return lax.broadcasted_iota(jnp.int32, shape, len(shape) - 1) < BLOCK


def prepare_kernel(where, places, *refs):
    *slots, out_ref, rows = refs
    left = left_half((HALF_ROW, LANES))
    down, across = (lax.broadcasted_iota(jnp.int32, (LANES, LANES), dim) for dim in range(2))
    unit = jnp.where(down == across, 1.0, 0.0).astype(jnp.bfloat16)
    for chunk in range(AT_ONCE):
        for row in range(SUB):
            for pair in range(PAIRS):
                first = slots[2 * pair][0, chunk, :, row, :]
                last = 2 * pair + 1 == SLOTS
                second = first if last else slots[2 * pair + 1][0, chunk, :, row, :]
                even = jnp.where(left, first, pltpu.roll(second, BLOCK, 1))
                odd = jnp.where(left, pltpu.roll(first, BLOCK, 1), second)
                slot = (chunk * SUB + row) * PAIRS + pair
                rows[slot, pl.ds(0, HALF_ROW, stride=2), :] = even
                rows[slot, pl.ds(1, HALF_ROW, stride=2), :] = odd
                depth = BLOCK if last else LANES
                turned = lax.dot_general(
                    unit[0:depth],
                    jnp.concatenate(split(rows[slot]), axis=0),
                    (((1,), (1,)), ((), ())),
                    preferred_element_type=jnp.float32,
                )
                out_ref[chunk, row, pl.ds(pair * LANES, depth), :] = turned.astype(jnp.bfloat16)


def slot_spec(slot):
    return pl.BlockSpec((1, AT_ONCE, HALF_ROW, SUB, LANES), lambda g: (slot, g, 0, 0, 0))


def prepare(where, places, coupling):
    raw = coupling.reshape(CHUNKS, SUB, SLOTS, HALF_ROW, LANES).transpose(2, 0, 3, 1, 4)
    raw = pltpu.with_memory_space_constraint(raw, pltpu.HBM)
    return pl.pallas_call(
        prepare_kernel,
        grid=(CHUNKS // AT_ONCE,),
        in_specs=[IN_SMEM, IN_SMEM] + [slot_spec(slot) for slot in range(SLOTS)],
        out_specs=pl.BlockSpec((AT_ONCE, SUB, DEPTH, LANES), lambda g: (g, 0, 0, 0)),
        out_shape=pltpu.HBM((CHUNKS, SUB, DEPTH, LANES), jnp.bfloat16),
        scratch_shapes=[pltpu.VMEM((AT_ONCE * SUB * PAIRS, BLOCK, LANES), jnp.float32)],
        compiler_params=pltpu.CompilerParams(vmem_limit_bytes=16 << 20),
        cost_estimate=pl.CostEstimate(flops=20_000_000_000, bytes_accessed=21 << 20, transcendentals=0),
        name="prepare",
    )(where, places, *[raw] * SLOTS)


def fill_picks(half, ref, picks):
    for chip in range(CHIPS):
        for tile in range(TILES):
            value = ref[chip, :, pl.ds(tile * LANES, LANES)]
            place = (half * CHIPS + chip) * PER_PIECE + 2 * tile
            for turn, turned in enumerate((value, pltpu.roll(value, BLOCK, 1))):
                high, low = split(turned)
                picks[place + turn, 0:MODES, :] = high
                picks[place + turn, MODES : 2 * MODES, :] = low


def fill_kernel(mine, picks):
    fill_picks(0, mine, picks)


def multiply(chunks, stores, places, picks, mats):
    left_picks = left_half((2 * MODES, LANES))
    left_out = left_half((MODES, LANES))
    for chunk, store in zip(chunks, stores):
        previous = None
        for offset in range(SUB):
            row = chunk * SUB + offset
            parts = []
            for pair in range(PAIRS):
                part = picks[places[2 * pair, row]]
                if 2 * pair + 1 < SLOTS:
                    parts.append(jnp.where(left_picks, part, picks[places[2 * pair + 1, row] ^ 1]))
                else:
                    parts.append(part[:, 0:BLOCK])
            product = jnp.dot(jnp.concatenate(parts, axis=1), mats[chunk, offset], preferred_element_type=jnp.float32)
            both = product[0:MODES] + product[MODES : 2 * MODES]
            both = both + pltpu.roll(both, BLOCK, 1)
            if offset % 2 == 1:
                store(pl.ds(offset // 2 * LANES, LANES), jnp.where(left_out, previous, both))
            previous = both


def into(ref, *index):
    def store(lanes, value):
        ref[(*index, slice(None), lanes)] = value

    return store


def multiply_group(where, change, places, picks, mats, out):
    y, low = (where[k] if same == 0 else 1 - where[k] for k, same in enumerate(change))
    chunks = [(y * Z_HI + a) * Z_LO + low for a in range(Z_HI)]
    multiply(chunks, [into(out, a) for a in range(Z_HI)], places, picks, mats)


def first_kernel(change, where, places, half_filled, other, mats, out, picks):
    fill_picks(1, other, picks)
    multiply_group(where, change, places, picks, mats, out)


def next_kernel(change, where, places, picks, mats, out):
    multiply_group(where, change, places, picks, mats, out)


def multiplier(kernel, change, name, inputs, outs, **more):
    return call(
        functools.partial(kernel, change),
        name,
        [IN_SMEM, IN_SMEM] + [IN_VMEM] * (inputs + 1),
        outs,
        flops=100_000,
        **more,
    )


def sum_kernel(where, *refs):
    shares, outs = refs[:-Z_HI], refs[-Z_HI:]
    for ahead, out in enumerate(outs):
        chip = (where[2] + ahead) % Z_HI
        total = shares[0][chip]
        for share in shares[1:]:
            total = total + share[chip]
        out[...] = total


def finish_kernel(scale, energies, vector, before, *refs):
    pieces, (out, *copies) = refs[:Z_HI], refs[Z_HI:]
    total = energies[...] * vector[...]
    for piece in pieces:
        total = total + piece[...]
    if scale != 1.0:
        total = scale * total - before[...]
    out[...] = total
    for ref in copies:
        for chip in range(CHIPS):
            ref[chip] = total


def tie_kernel(mine, mats, out):
    pass


def swap(value, axis):
    return lax.ppermute(value, axis, [(0, 1), (1, 0)])


def shift(value, by):
    return lax.ppermute(value, "z_hi", [(k, (k + by) % Z_HI) for k in range(Z_HI)])


def exchange(value, change):
    pairs = []
    for k in range(Y_HI * Z_LO):
        y, low = k // Z_LO, k % Z_LO
        pairs.append((k, (y ^ change[0]) * Z_LO + (low ^ change[1])))
    return lax.ppermute(value, ("y_hi", "z_lo"), pairs)


def shards(start_modes, energies, coupling, pattern):
    core, y_hi, z_lo = (lax.axis_index(name) for name in ("core", "y_hi", "z_lo"))
    turned = pattern.T
    piece_row = turned // (PER_PIECE * CHUNKS)
    places = (((piece_row % CORE) ^ core) * CHIPS + piece_row // CORE) * PER_PIECE + turned % PER_PIECE
    where = jnp.stack([y_hi, z_lo, lax.axis_index("z_hi")]).astype(jnp.int32)
    mats = prepare(where, places, coupling)
    level = energies[None, :]
    picks_shape = kept_in_vmem(ROWS_HERE, 2 * MODES, LANES, dtype=jnp.bfloat16)
    vector_shape = kept_in_vmem(MODES, PIECE)
    share_shape = kept_in_vmem(Z_HI, MODES, PIECE)

    def operate(copies, tied):
        mine = lax.all_to_all(copies, ("y_lo", "x"), 0, 0, tiled=False)
        if tied:
            [mine] = call(
                tie_kernel, "tie", [IN_VMEM, pl.BlockSpec(memory_space=pl.ANY)], [kept_in_vmem(*mine.shape)], input_output_aliases={0: 0}
            )(mine, pltpu.with_memory_space_constraint(mats, pltpu.HBM))
        other = swap(mine, "core")
        changes = ((1, 1), (1, 0), (0, 1), (0, 0))
        [picks] = call(fill_kernel, "fill", [IN_VMEM], [picks_shape])(mine)
        share, picks = multiplier(
            first_kernel, changes[0], "first", 2, [share_shape, picks_shape], input_output_aliases={2: 1}
        )(where, places, picks, other, mats)
        got = [exchange(share, changes[0])]
        for change in changes[1:]:
            [share] = multiplier(next_kernel, change, "next", 1, [share_shape])(where, places, picks, mats)
            got.append(exchange(share, change) if any(change) else share)
        sums = call(
            sum_kernel,
            "sum",
            [IN_SMEM] + [IN_VMEM] * len(got),
            [vector_shape] * Z_HI,
        )(where, *got)
        return [sums[0]] + [shift(sums[by], by) for by in (2, 1, 3)]

    previous = before = start_modes
    current = start_modes
    copies = jnp.broadcast_to(start_modes[None], (CHIPS, MODES, PIECE))
    for degree in range(DEGREE):
        pieces = operate(copies, degree == 0)
        finish = functools.partial(finish_kernel, 1.0 if degree == 0 else 2.0)
        outs = [vector_shape]
        if degree < DEGREE - 1:
            outs.append(kept_in_vmem(CHIPS, MODES, PIECE))
        upcoming, *rest = call(finish, "finish", [IN_VMEM] * (3 + Z_HI), outs)(level, current, before, *pieces)
        copies = rest[0] if rest else None
        before = current
        current = upcoming
    return (current, before)


def solution(mesh):
    fine = Mesh(mesh.devices.reshape(Y_LO, X, CORE, Y_HI, Z_HI, Z_LO), ROW_AXES + COL_AXES)
    both = ROW_AXES + COL_AXES
    in_specs = (P(None, both), P(both), P(ROW_AXES, COL_AXES, None), P(ROW_AXES, COL_AXES))
    out_specs = (P(None, both), P(None, both))
    return jax.shard_map(shards, mesh=fine, in_specs=in_specs, out_specs=out_specs, check_vma=False)
```

```python
import functools

import jax
import jax.numpy as jnp
from jax import lax
from jax.experimental import pallas as pl
from jax.experimental.pallas import tpu as pltpu
from jax.sharding import Mesh
from jax.sharding import PartitionSpec as P

BLOCK = 64
DEGREE = 3
LANES = 128
SUB = 8
SLOTS = 5
PAIRS = (SLOTS + 1) // 2
DEPTH = SLOTS * BLOCK
MODES = 32
PER_PIECE = 8
PIECE = BLOCK * PER_PIECE
TILES = PIECE // LANES
ROWS_HERE = 128
HALF_ROW = BLOCK // 2
AT_ONCE = 4

Y_LO, X, CORE, Y_HI, Z_HI, Z_LO = 2, 4, 2, 2, 4, 2
CHIPS = Y_LO * X
Z = Z_HI * Z_LO
CHUNKS = Y_HI * Z
ROW_AXES = ("y_lo", "x", "core")
COL_AXES = ("y_hi", "z_hi", "z_lo")
IN_VMEM = pl.BlockSpec(memory_space=pltpu.VMEM)
IN_SMEM = pl.BlockSpec(memory_space=pltpu.SMEM)


def kept_in_vmem(*shape, dtype=jnp.float32):
    return pltpu.VMEM(shape, dtype)


def call(kernel, name, in_specs, outs, scratch=(), flops=1_000_000, mebibytes=8, **more):
    return pl.pallas_call(
        kernel,
        in_specs=in_specs,
        out_specs=[IN_VMEM] * len(outs),
        out_shape=list(outs),
        scratch_shapes=list(scratch),
        compiler_params=pltpu.CompilerParams(vmem_limit_bytes=mebibytes << 20),
        cost_estimate=pl.CostEstimate(flops=flops, bytes_accessed=100_000, transcendentals=0),
        name=name,
        **more,
    )


def split(value):
    high = value.astype(jnp.bfloat16)
    low = (value - high.astype(jnp.float32)).astype(jnp.bfloat16)
    return high, low


def left_half(shape):
    return lax.broadcasted_iota(jnp.int32, shape, len(shape) - 1) < BLOCK


def prepare_kernel(where, places, *refs):
    *slots, out_ref, rows = refs
    left = left_half((HALF_ROW, LANES))
    down, across = (lax.broadcasted_iota(jnp.int32, (LANES, LANES), dim) for dim in range(2))
    unit = jnp.where(down == across, 1.0, 0.0).astype(jnp.bfloat16)
    for chunk in range(AT_ONCE):
        for row in range(SUB):
            for pair in range(PAIRS):
                first = slots[2 * pair][0, chunk, :, row, :]
                last = 2 * pair + 1 == SLOTS
                second = first if last else slots[2 * pair + 1][0, chunk, :, row, :]
                even = jnp.where(left, first, pltpu.roll(second, BLOCK, 1))
                odd = jnp.where(left, pltpu.roll(first, BLOCK, 1), second)
                slot = (chunk * SUB + row) * PAIRS + pair
                rows[slot, pl.ds(0, HALF_ROW, stride=2), :] = even
                rows[slot, pl.ds(1, HALF_ROW, stride=2), :] = odd
                depth = BLOCK if last else LANES
                turned = lax.dot_general(
                    unit[0:depth],
                    jnp.concatenate(split(rows[slot]), axis=0),
                    (((1,), (1,)), ((), ())),
                    preferred_element_type=jnp.float32,
                )
                out_ref[chunk, row, pl.ds(pair * LANES, depth), :] = turned.astype(jnp.bfloat16)


def slot_spec(slot):
    return pl.BlockSpec((1, AT_ONCE, HALF_ROW, SUB, LANES), lambda g: (slot, g, 0, 0, 0))


def prepare(where, places, coupling):
    raw = coupling.reshape(CHUNKS, SUB, SLOTS, HALF_ROW, LANES).transpose(2, 0, 3, 1, 4)
    raw = pltpu.with_memory_space_constraint(raw, pltpu.HBM)
    return pl.pallas_call(
        prepare_kernel,
        grid=(CHUNKS // AT_ONCE,),
        in_specs=[IN_SMEM, IN_SMEM] + [slot_spec(slot) for slot in range(SLOTS)],
        out_specs=pl.BlockSpec((AT_ONCE, SUB, DEPTH, LANES), lambda g: (g, 0, 0, 0)),
        out_shape=pltpu.HBM((CHUNKS, SUB, DEPTH, LANES), jnp.bfloat16),
        scratch_shapes=[pltpu.VMEM((AT_ONCE * SUB * PAIRS, BLOCK, LANES), jnp.float32)],
        compiler_params=pltpu.CompilerParams(vmem_limit_bytes=16 << 20),
        cost_estimate=pl.CostEstimate(flops=20_000_000_000, bytes_accessed=21 << 20, transcendentals=0),
        name="prepare",
    )(where, places, *[raw] * SLOTS)


def fill_picks(half, ref, picks):
    for chip in range(CHIPS):
        for tile in range(TILES):
            value = ref[chip, :, pl.ds(tile * LANES, LANES)]
            place = (half * CHIPS + chip) * PER_PIECE + 2 * tile
            for turn, turned in enumerate((value, pltpu.roll(value, BLOCK, 1))):
                high, low = split(turned)
                picks[place + turn, 0:MODES, :] = high
                picks[place + turn, MODES : 2 * MODES, :] = low


def fill_kernel(mine, picks):
    fill_picks(0, mine, picks)


def multiply(chunks, stores, places, picks, mats):
    left_picks = left_half((2 * MODES, LANES))
    left_out = left_half((MODES, LANES))
    for chunk, store in zip(chunks, stores):
        previous = None
        for offset in range(SUB):
            row = chunk * SUB + offset
            parts = []
            for pair in range(PAIRS):
                part = picks[places[2 * pair, row]]
                if 2 * pair + 1 < SLOTS:
                    parts.append(jnp.where(left_picks, part, picks[places[2 * pair + 1, row] ^ 1]))
                else:
                    parts.append(part[:, 0:BLOCK])
            product = jnp.dot(jnp.concatenate(parts, axis=1), mats[chunk, offset], preferred_element_type=jnp.float32)
            both = product[0:MODES] + product[MODES : 2 * MODES]
            both = both + pltpu.roll(both, BLOCK, 1)
            if offset % 2 == 1:
                store(pl.ds(offset // 2 * LANES, LANES), jnp.where(left_out, previous, both))
            previous = both


def into(ref, *index):
    def store(lanes, value):
        ref[(*index, slice(None), lanes)] = value

    return store


def multiply_group(where, change, places, picks, mats, out):
    y, low = (where[k] if same == 0 else 1 - where[k] for k, same in enumerate(change))
    chunks = [(y * Z_HI + a) * Z_LO + low for a in range(Z_HI)]
    multiply(chunks, [into(out, a) for a in range(Z_HI)], places, picks, mats)


def first_kernel(change, where, places, half_filled, other, mats, out, picks):
    fill_picks(1, other, picks)
    multiply_group(where, change, places, picks, mats, out)


def next_kernel(change, where, places, picks, mats, out):
    multiply_group(where, change, places, picks, mats, out)


def multiplier(kernel, change, name, inputs, outs, **more):
    return call(
        functools.partial(kernel, change),
        name,
        [IN_SMEM, IN_SMEM] + [IN_VMEM] * (inputs + 1),
        outs,
        flops=100_000,
        **more,
    )


def sum_kernel(where, *refs):
    shares, outs = refs[:-Z_HI], refs[-Z_HI:]
    for ahead, out in enumerate(outs):
        chip = (where[2] + ahead) % Z_HI
        total = shares[0][chip]
        for share in shares[1:]:
            total = total + share[chip]
        out[...] = total


def finish_kernel(scale, energies, vector, before, *refs):
    pieces, (out, *copies) = refs[:Z_HI], refs[Z_HI:]
    total = energies[...] * vector[...]
    for piece in pieces:
        total = total + piece[...]
    if scale != 1.0:
        total = scale * total - before[...]
    out[...] = total
    for ref in copies:
        for chip in range(CHIPS):
            ref[chip] = total


def tie_kernel(mine, mats, out):
    pass


def swap(value, axis):
    return lax.ppermute(value, axis, [(0, 1), (1, 0)])


def shift(value, by):
    return lax.ppermute(value, "z_hi", [(k, (k + by) % Z_HI) for k in range(Z_HI)])


def exchange(value, change):
    pairs = []
    for k in range(Y_HI * Z_LO):
        y, low = k // Z_LO, k % Z_LO
        pairs.append((k, (y ^ change[0]) * Z_LO + (low ^ change[1])))
    return lax.ppermute(value, ("y_hi", "z_lo"), pairs)


def shards(start_modes, energies, coupling, pattern):
    core, y_hi, z_lo = (lax.axis_index(name) for name in ("core", "y_hi", "z_lo"))
    turned = pattern.T
    piece_row = turned // (PER_PIECE * CHUNKS)
    places = (((piece_row % CORE) ^ core) * CHIPS + piece_row // CORE) * PER_PIECE + turned % PER_PIECE
    where = jnp.stack([y_hi, z_lo, lax.axis_index("z_hi")]).astype(jnp.int32)
    mats = prepare(where, places, coupling)
    level = energies[None, :]
    picks_shape = kept_in_vmem(ROWS_HERE, 2 * MODES, LANES, dtype=jnp.bfloat16)
    vector_shape = kept_in_vmem(MODES, PIECE)
    share_shape = kept_in_vmem(Z_HI, MODES, PIECE)

    def operate(copies, tied):
        mine = lax.all_to_all(copies, ("y_lo", "x"), 0, 0, tiled=False)
        if tied:
            [mine] = call(
                tie_kernel, "tie", [IN_VMEM, pl.BlockSpec(memory_space=pl.ANY)], [kept_in_vmem(*mine.shape)], input_output_aliases={0: 0}
            )(mine, pltpu.with_memory_space_constraint(mats, pltpu.HBM))
        other = swap(mine, "core")
        changes = ((1, 1), (1, 0), (0, 1), (0, 0))
        [picks] = call(fill_kernel, "fill", [IN_VMEM], [picks_shape])(mine)
        share, picks = multiplier(
            first_kernel, changes[0], "first", 2, [share_shape, picks_shape], input_output_aliases={2: 1}
        )(where, places, picks, other, mats)
        got = [exchange(share, changes[0])]
        for change in changes[1:]:
            [share] = multiplier(next_kernel, change, "next", 1, [share_shape])(where, places, picks, mats)
            got.append(exchange(share, change) if any(change) else share)
        sums = call(
            sum_kernel,
            "sum",
            [IN_SMEM] + [IN_VMEM] * len(got),
            [vector_shape] * Z_HI,
        )(where, *got)
        return [sums[0]] + [shift(sums[by], by) for by in (2, 1, 3)]

    previous = before = start_modes
    current = start_modes
    copies = jnp.broadcast_to(start_modes[None], (CHIPS, MODES, PIECE))
    for degree in range(DEGREE):
        pieces = operate(copies, degree == 0)
        finish = functools.partial(finish_kernel, 1.0 if degree == 0 else 2.0)
        outs = [vector_shape]
        if degree < DEGREE - 1:
            outs.append(kept_in_vmem(CHIPS, MODES, PIECE))
        upcoming, *rest = call(finish, "finish", [IN_VMEM] * (3 + Z_HI), outs)(level, current, before, *pieces)
        copies = rest[0] if rest else None
        before = current
        current = upcoming
    return (current, before)


def solution(mesh):
    fine = Mesh(mesh.devices.reshape(Y_LO, X, CORE, Y_HI, Z_HI, Z_LO), ROW_AXES + COL_AXES)
    both = ROW_AXES + COL_AXES
    in_specs = (P(None, both), P(both), P(ROW_AXES, COL_AXES, None), P(ROW_AXES, COL_AXES))
    out_specs = (P(None, both), P(None, both))
    return jax.shard_map(shards, mesh=fine, in_specs=in_specs, out_specs=out_specs, check_vma=False)
```
